32 devices in a mesh: grp: 8 (over z, y), col: 4 (over x, core).
Axes of the slice: x: 2, y: 2, z: 4, core: 2. Of those that a mesh axis runs over, the one named last changes fastest.
Arguments:
- window_rows: bfloat16 [122880, 1024], P('grp', 'col'), may hold values from -0.0234375 to 0.0234375
- secular: bfloat16 [122880, 4096], P('grp', 'col'), may hold values from -6 to 6
- source: int32 [122880], P('grp'), may hold values from 0 to 122879, as said below
- kept_count: int32 [1], replicated, may hold values from 61440 to 122879
Outputs:
- merged: bfloat16 [2, 1024, 4096], P(None, 'grp', 'col')
The draws below stay inside these ranges and needn't reach their ends.
Inputs may be any that keep to these rules, and one draw needn't show every extreme that they name: source is a permutation of 0 to 122879; for j in block b of 15360 indices, source[j] lies in block b or in block b + 4 (b < 4) or b - 4 (b >= 4).
All inputs are finite; a program needn't handle non-finite values.
Results may differ from the reference program's by a relative error of at most 0.0011.
Values may be sent and summed in bfloat16 or wider, within the bound.
A program may use at most 256 MiB of HBM per device.

```python
import jax
import jax.numpy as jnp
from jax import lax

N = 122880
RH = 1024
KS = 4096
BLK = 15360
PAIRS = 4


def draw_source(key, part):
    key = jax.random.fold_in(key, 7)
    counts = jax.random.randint(jax.random.fold_in(key, 1), (PAIRS,), 0, BLK + 1).astype(jnp.int32)
    chosen = jax.random.permutation(jax.random.fold_in(key, 2), PAIRS)
    counts = counts.at[chosen[0]].set(BLK).at[chosen[1]].set(0)
    positions = jnp.arange(BLK, dtype=jnp.int32)

    def one_pair(index, count):
        pair_key = jax.random.fold_in(jax.random.fold_in(key, 3), index)
        order_a = jax.random.permutation(jax.random.fold_in(pair_key, 1), BLK).astype(jnp.int32)
        order_b = jax.random.permutation(jax.random.fold_in(pair_key, 2), BLK).astype(jnp.int32)
        shuffle_a = jax.random.permutation(jax.random.fold_in(pair_key, 3), BLK).astype(jnp.int32)
        shuffle_b = jax.random.permutation(jax.random.fold_in(pair_key, 4), BLK).astype(jnp.int32)
        base_a = index * BLK
        base_b = (index + PAIRS) * BLK
        crossing = positions < count
        list_a = jnp.where(crossing, base_b + order_b, base_a + order_a)
        list_b = jnp.where(crossing, base_a + order_a, base_b + order_b)
        return jnp.concatenate([list_a[shuffle_a], list_b[shuffle_b]]).astype(jnp.int32)
    paired = jax.vmap(one_pair)(jnp.arange(PAIRS, dtype=jnp.int32), counts)
    first = paired[:, :BLK].reshape(-1)
    second = paired[:, BLK:].reshape(-1)
    return jnp.concatenate([first, second]).astype(jnp.int32)


def level_of(key, extent, split, low, largest):
    def one(dim, shards_of):
        draws = jax.random.uniform(jax.random.fold_in(jax.random.fold_in(key, 6), dim), (shards_of,), jnp.float32, low / len(split), largest / len(split))
        return jnp.repeat(jnp.exp(draws), extent[dim] // shards_of).reshape((-1,) + (1,) * (len(extent) - dim - 1))

    loudness = one(*split[0])
    for cut in split[1:]:
        loudness = loudness * one(*cut)
    return loudness


def normal_values(key, extent, deviation, most, cuts=(), held_as=jnp.bfloat16):
    values = jax.random.normal(key, extent, jnp.float32) * deviation
    if len(cuts) > 0:
        values = level_of(key, extent, cuts, -0.22, 0.18) * values
    return jnp.clip(values, min=-most, max=most).astype(held_as)


def setup_inputs(seed: int = 0) -> dict:
    key_list = jax.random.split(jax.random.key(seed), 5)
    return {
        "window_rows": normal_values(key_list[0], (N, RH), (N // 2) ** -0.5, 0.0234375, ((0, 8), (1, 4))),
        "secular": normal_values(key_list[1], (N, KS), 1.0, 6.0, ((0, 8), (1, 4))),
        "source": draw_source(jax.random.fold_in(key_list[4], 71), 0),
        "kept_count": jax.random.randint(key_list[3], (1,), N // 2, N).astype(jnp.int32),
    }


def reference(window_rows, secular, source, kept_count):
    limit = kept_count[0]
    valid = source < limit
    half = N // 2
    width = min(KS, 512)

    def one_block(index):
        columns = lax.dynamic_slice_in_dim(secular, index * width, width, 1)
        picked = jnp.where(valid[:, None], columns[source], jnp.zeros((), jnp.bfloat16))
        upper = jnp.dot(window_rows[:half].T, picked[:half], preferred_element_type=jnp.float32)
        lower = jnp.dot(window_rows[half:].T, picked[half:], preferred_element_type=jnp.float32)
        return jnp.stack([upper, lower])

    blocks = lax.map(one_block, jnp.arange(KS // width, dtype=jnp.int32))
    return blocks.transpose(1, 2, 0, 3).reshape(2, RH, KS).astype(jnp.bfloat16)
```

```python
import functools

import jax
import jax.numpy as jnp
from jax import lax
from jax.experimental import pallas as pl
from jax.experimental.pallas import tpu as pltpu
from jax.sharding import PartitionSpec as P

UNROLL = 16
TILE = 64


def partner_2(value, axis, bit):
    mask = 2**bit
    pairs = [(source, source ^ mask) for source in range(lax.axis_size(axis))]
    return lax.ppermute(value, axis, pairs)


def invert_kernel(blk, base_ref, own_ref, partner_ref, inverse_ref):
    base = base_ref[0]

    def run(source_ref, first):
        def body(step, carry):
            for k in range(UNROLL):
                j = step * UNROLL + k
                place = source_ref[j] - base
                inside = (place >= 0) & (place < blk)
                inverse_ref[jnp.where(inside, place, blk)] = j + first
            return carry

        lax.fori_loop(0, blk // UNROLL, body, 0)

    run(own_ref, 0)
    run(partner_ref, blk)


def invert(base, own_source, partner_source):
    blk = own_source.shape[0]
    smem = pl.BlockSpec(memory_space=pltpu.SMEM)
    inverse = pl.pallas_call(
        functools.partial(invert_kernel, blk),
        out_shape=jax.ShapeDtypeStruct((blk + 128,), jnp.int32),
        in_specs=[smem] * 3,
        out_specs=smem,
        cost_estimate=pl.CostEstimate(flops=8 * blk, bytes_accessed=12 * blk, transcendentals=0),
    )(base.reshape(1), own_source, partner_source)
    return inverse[:blk]


def pick_kernel(blk, inverse_ref, own_ref, partner_ref, out_ref, wide_ref, stage_ref):
    def widen(step, carry):
        rows = pl.ds(pl.multiple_of(step * 256, 256), 256)
        wide_ref[rows, :] = own_ref[rows, :].astype(jnp.float32)
        wide_ref[pl.ds(pl.multiple_of(blk + step * 256, 256), 256), :] = partner_ref[rows, :].astype(jnp.float32)
        return carry

    lax.fori_loop(0, blk // 256, widen, 0)

    def pick(step, carry):
        first = pl.multiple_of(step * TILE, TILE)
        for k in range(TILE):
            stage_ref[pl.ds(k, 1), :] = wide_ref[pl.ds(inverse_ref[first + k], 1), :]
        out_ref[pl.ds(first, TILE), :] = stage_ref[...].astype(out_ref.dtype)
        return carry

    lax.fori_loop(0, blk // TILE, pick, 0)


def pick_rows(inverse, own, partner):
    blk, wide = own.shape
    vmem = pl.BlockSpec(memory_space=pltpu.VMEM)
    return pl.pallas_call(
        functools.partial(pick_kernel, blk),
        out_shape=jax.ShapeDtypeStruct((blk, wide), own.dtype),
        in_specs=[pl.BlockSpec(memory_space=pltpu.SMEM), vmem, vmem],
        out_specs=vmem,
        scratch_shapes=[
            pltpu.VMEM((2 * blk, wide), jnp.float32),
            pltpu.VMEM((TILE, wide), jnp.float32),
        ],
        compiler_params=pltpu.CompilerParams(vmem_limit_bytes=40 * 2**20),
        cost_estimate=pl.CostEstimate(flops=2 * blk * wide, bytes_accessed=64 * blk * wide, transcendentals=0),
    )(inverse, own, partner)


def scatter_sum(terms):
    return lax.psum_scatter(jnp.stack(terms), "grp", scatter_dimension=1, tiled=True)


def per_device(window_rows, secular, source, kept_count):
    blk, wide = window_rows.shape
    groups = lax.axis_size("grp")
    halves = 2
    half_bit = groups.bit_length() - 2
    group_index = lax.axis_index("grp")
    half_index = group_index // (groups // 2)
    base = group_index * blk

    owners = groups // lax.axis_size("col")
    chunks = 2 if wide >= 256 else 1
    share = wide // owners // chunks
    own = [
        jnp.concatenate(
            [window_rows[:, (o * chunks + k) * share : (o * chunks + k + 1) * share] for o in range(owners)],
            axis=1,
        )
        for k in range(chunks)
    ]

    partner_source = partner_2(source, "grp", half_bit)
    partner = []
    for k in range(chunks):
        sent = own[k]
        if k > 0:
            sent, partner[k - 1] = lax.optimization_barrier((sent, partner[k - 1]))
        partner.append(partner_2(sent, "grp", half_bit))

    inverse = invert(base, source, partner_source)
    crossed = inverse >= blk
    kept = (base + jnp.arange(blk, dtype=jnp.int32)) < kept_count[0]
    masks = [kept & (crossed == (half_index != half)) for half in range(halves)]

    parts = []
    for k in range(chunks):
        arrived = partner[k]
        if k > 0:
            arrived, terms = lax.optimization_barrier((arrived, terms))
            parts.append(scatter_sum(terms))
        picked = pick_rows(inverse, own[k], arrived)
        rows = lax.all_gather(picked, "col", axis=1, tiled=True)
        terms = [
            lax.dot_general(
                jnp.where(mask[:, None], rows, jnp.zeros((), rows.dtype)),
                secular,
                (((0,), (0,)), ((), ())),
                preferred_element_type=jnp.float32,
            )
            for mask in masks
        ]
    parts.append(scatter_sum(terms))
    return jnp.concatenate(parts, axis=1).astype(jnp.bfloat16)


def solution(mesh):
    return jax.shard_map(
        per_device,
        mesh=mesh,
        in_specs=(P("grp", "col"), P("grp", "col"), P("grp"), P()),
        out_specs=P(None, "grp", "col"),
        check_vma=False,
    )
```
